32 devices in a mesh: ep: 16 (over z, x, core), tp: 2 (over y).
Axes of the slice: x: 2, y: 2, z: 4, core: 2. Of those that a mesh axis runs over, the one named last changes fastest.
Arguments:
- tokens: bfloat16 [2048, 7168], P(('ep', 'tp')), may hold values from -6 to 6
- expert_ids: int32 [2048, 8], P(('ep', 'tp')), may hold values from 0 to 15, all different within a row; in each aligned block of 64 rows (0 to 63, 64 to 127, ...) at most 64 rows name the same one
- gate_fixed: int32 [2048, 8], P(('ep', 'tp')), may hold values from 4096 to 32767
- expert_weights: bfloat16 [16, 3, 7168, 1024], P('ep', None, None, 'tp'), may hold values from -0.125 to 0.125
- shared_weights: bfloat16 [3, 7168, 1024], P(None, None, 'tp'), may hold values from -0.125 to 0.125
Outputs:
- mixed: bfloat16 [2048, 7168], P(('ep', 'tp'))
The draws below stay inside these ranges and needn't reach their ends.
Inputs may be any that keep to these rules, and one draw needn't show every extreme that they name: `expert_ids`: each row names 8 different experts. In the 64 rows of one device no expert is named by more than 64 rows.
All inputs are finite; a program needn't handle non-finite values.
Results may differ from the reference program's by a relative error of at most 0.0075.
Values may be sent and summed in bfloat16 or wider, within the bound.
A program may use at most 128 MiB of HBM per device.

```python
import math
import jax
import jax.numpy as jnp
import numpy as np
from jax import lax

D = 7168
FF = 1024
SFF = 1024
TOP = 8
CAP = 8
TOK_DEV = 64
EXPERTS = 16
MOST = 64
TOKENS = 2048
N_EP = 16
N_TP = 2


def set_ends(drawn, key, low, top_value):
    index_at = [jax.random.randint(jax.random.fold_in(key, axis), (), 0, length) for axis, length in enumerate(drawn.shape)]
    widest = drawn.shape.index(max(drawn.shape))
    neighbour = index_at[:widest] + [(index_at[widest] + 1) % drawn.shape[widest]] + index_at[widest + 1:]
    return drawn.at[tuple(index_at)].set(low).at[tuple(neighbour)].set(top_value)


def block_scale(key, shape, pieces, smallest, high):
    def one(axis_at, blocks):
        heights = jax.random.uniform(jax.random.fold_in(jax.random.fold_in(key, 6), axis_at), (blocks,), jnp.float32, smallest / len(pieces), high / len(pieces))
        return jnp.repeat(jnp.exp(heights), shape[axis_at] // blocks).reshape((-1,) + (1,) * (len(shape) - axis_at - 1))

    loudness = one(*pieces[0])
    for cut in pieces[1:]:
        loudness = loudness * one(*cut)
    return loudness


def assign_block(own_key, own, number, rows, number_of, top, limit, skew):
    sequence = jax.random.permutation(own_key, number_of)
    crowded, common = load_shares(number_of, rows * top, limit, skew, True), load_shares(number_of, rows * top, limit, skew, False)
    places = jnp.arange(number_of)

    def named(sizes, turn):
        used = int((sizes > 0).sum())
        fixed = max(1, used // 4)
        passed = fixed + (places - fixed + turn * (used - fixed)) % max(1, number_of - fixed)
        return jnp.zeros((number_of,), jnp.int32).at[sequence[jnp.where(places < fixed, places, passed)]].set(jnp.asarray(sizes, jnp.int32))

    sizes = jnp.where(number % 4 == 0, named(crowded, number // 4), named(common, number - number // 4 - 1))
    mixed = jax.random.permutation(jax.random.fold_in(own, 3), number_of)
    giver, taker = mixed[0:number_of // 2 * 2:2], mixed[1:number_of // 2 * 2:2]
    slack = jnp.minimum(sizes[giver] - 1, limit - sizes[taker]) // 2
    slack = jnp.where((giver == sequence[0]) | (taker == sequence[0]) | (sizes[taker] == 0), 0, jnp.maximum(slack, 0))
    passed = jax.random.randint(jax.random.fold_in(own, 4), (number_of // 2,), 0, 1 << 20) % (slack + 1)
    sizes = sizes.at[giver].add(-passed).at[taker].add(passed)
    members = jnp.searchsorted(jnp.cumsum(sizes), jnp.arange(rows * top), side="right").astype(jnp.int32)
    listing = members.reshape(top, rows).T
    listing = listing[jax.random.permutation(jax.random.fold_in(own, 1), rows)]
    turn = jax.random.randint(jax.random.fold_in(own, 2), (rows, 1), 0, top)
    return jnp.take_along_axis(listing, (jnp.arange(top)[None, :] + turn) % top, axis=1)


def load_shares(count, total, reach, skew, full):
    loads = [(1 << 20) // math.isqrt(rank ** skew) + 1 for rank in range(1, count + 1)]
    largest = reach if full else min(reach, max(-(-total // count), total * loads[0] // sum(loads)))
    least = 1 if total - largest >= count - 1 else 0
    given, surplus = [largest] + [least] * (count - 1), total - largest - least * (count - 1)
    while surplus > 0:
        movable = [i for i in range(1, count) if given[i] < largest] or [i for i in range(1, count) if given[i] < reach]
        whole, left = sum([loads[i] for i in movable]), surplus
        for i in movable:
            addition = min(reach - given[i], max(1, left * loads[i] // whole), surplus)
            given[i] = given[i] + addition
            surplus = surplus - addition
    return np.array(given)


def noise(key, shape, scale, most, cuts=(), kind=jnp.bfloat16):
    level = block_scale(key, shape, cuts, -0.22, 0.18) if cuts else 1.0
    values = jax.random.normal(key, shape, jnp.float32) * scale * level
    return jnp.minimum(jnp.maximum(values, -most), most).astype(kind)


def setup_inputs(seed: int = 0) -> dict:
    arg_keys = jax.random.split(jax.random.key(seed), 6)
    tokens = noise(arg_keys[0], (TOKENS, D), 1.0, 6.0, ((0, 32),))
    expert_ids_keys = jax.random.split(jax.random.fold_in(arg_keys[1], 1), TOKENS // TOK_DEV)
    expert_ids_turns = jax.random.permutation(jax.random.fold_in(arg_keys[1], 3), TOKENS // TOK_DEV)
    expert_ids = jax.vmap(lambda own, number: assign_block(jax.random.fold_in(arg_keys[1], 2), own, number, TOK_DEV, EXPERTS, TOP, MOST, 2))(expert_ids_keys, expert_ids_turns).reshape((TOKENS, TOP))
    gate_fixed = set_ends(jax.random.randint(arg_keys[2], (TOKENS, TOP), 4096, 32768), jax.random.fold_in(arg_keys[2], 1), 4096, 32767).astype(jnp.int32)
    expert_weights = noise(arg_keys[3], (EXPERTS, 3, D, FF), (2 * FF) ** -0.5, 0.125, ((0, 16), (3, 2)))
    shared_weights = noise(arg_keys[4], (3, D, SFF), (2 * SFF) ** -0.5, 0.125, ((2, 2),))
    return {"tokens": tokens, "expert_ids": expert_ids, "gate_fixed": gate_fixed, "expert_weights": expert_weights, "shared_weights": shared_weights}


def expert_apply(inputs, weights, parts):
    width = weights.shape[2] // parts
    total = jnp.zeros((inputs.shape[0], inputs.shape[1]), jnp.float32)
    for index in range(parts):
        block = weights[:, :, index * width:(index + 1) * width]
        gate_proj = jnp.dot(inputs, block[0], preferred_element_type=jnp.float32)
        up_proj = jnp.dot(inputs, block[1], preferred_element_type=jnp.float32)
        hidden = (jax.nn.silu(gate_proj) * up_proj).astype(jnp.bfloat16)
        partial_out = lax.dot_general(hidden, block[2], (((1,), (1,)), ((), ())), preferred_element_type=jnp.float32)
        rounded = lax.optimization_barrier(partial_out.astype(jnp.bfloat16))
        total = total + rounded.astype(jnp.float32)
    return total


def reference(tokens, expert_ids, gate_fixed, expert_weights, shared_weights):
    devices_all = N_EP * N_TP
    per_dev = TOKENS // devices_all
    width = tokens.shape[1]
    expert_range = jnp.arange(EXPERTS, dtype=jnp.int32)
    match = expert_ids[:, :, None] == expert_range[None, None, :]
    member = jnp.sum(match.astype(jnp.int32), axis=1)
    gate_value = jnp.sum(jnp.where(match, gate_fixed[:, :, None], 0), axis=1).astype(jnp.float32) / 65536.0
    member_dev = member.reshape(devices_all, per_dev, EXPERTS)
    position = jnp.cumsum(member_dev, axis=1) - member_dev
    kept = member_dev * (position < CAP).astype(jnp.int32)
    slot_range = jnp.arange(CAP, dtype=jnp.int32)
    hit = (kept[..., None] == 1) & (position[..., None] == slot_range[None, None, None, :])
    row_range = jnp.arange(per_dev, dtype=jnp.int32)
    slot_token = jnp.sum(jnp.where(hit, row_range[None, :, None, None], 0), axis=1).astype(jnp.int32)
    valid = jnp.any(hit, axis=1)
    token_dev = tokens.reshape(devices_all, per_dev, width)
    picked = jax.vmap(lambda source, index: source[index])(token_dev, slot_token)
    picked = jnp.where(valid[..., None], picked, jnp.zeros_like(picked))
    by_expert = jnp.transpose(picked, (1, 0, 2, 3))

    def run_expert(pair):
        expert_input, weights = pair
        result = expert_apply(expert_input.reshape(-1, width), weights, N_TP)
        return result.astype(jnp.bfloat16).reshape(devices_all, CAP, width)

    expert_out = lax.map(run_expert, (by_expert, expert_weights))
    returned = jnp.transpose(expert_out, (1, 0, 2, 3))
    combine = (hit.astype(jnp.float32) * gate_value.reshape(devices_all, per_dev, EXPERTS)[..., None])

    def combine_dev(pair):
        weights_dev, values_dev = pair
        return jnp.dot(weights_dev.reshape(per_dev, EXPERTS * CAP), values_dev.reshape(EXPERTS * CAP, width).astype(jnp.float32), precision=lax.Precision.HIGHEST)

    routed = lax.map(combine_dev, (combine, returned)).reshape(TOKENS, width)
    shared = expert_apply(tokens, shared_weights, N_TP)
    return (shared + routed).astype(jnp.bfloat16)
```

```python
import functools

import jax
import jax.numpy as jnp
from jax import lax
from jax.experimental import pallas as pl
from jax.experimental.pallas import tpu as pltpu
from jax.sharding import PartitionSpec as P

CAP = 8
MESH = pl.DeviceIdType.MESH
BF16 = jnp.bfloat16
F32 = jnp.float32

SPANS = 2
PIECES = 4
STEP = 256
DEPTH = 1024


def dot(a, b):
    return jnp.dot(a, b, preferred_element_type=F32)


def dot_t(a, b):
    return lax.dot_general(a, b, (((1,), (1,)), ((), ())), preferred_element_type=F32)


def routing(meta, experts):
    tops = meta.shape[0] // 2
    both = meta.shape[1]
    expert = lax.broadcasted_iota(jnp.int32, (experts, both), 0)
    member = jnp.zeros((experts, both), F32)
    high = jnp.zeros((experts, both), F32)
    low = jnp.zeros((experts, both), F32)
    for k in range(tops):
        match = meta[k : k + 1, :] == expert
        gate = meta[tops + k : tops + k + 1, :]
        member += jnp.where(match, 1.0, 0.0)
        high += jnp.where(match, (gate >> 8).astype(F32), 0.0)
        low += jnp.where(match, (gate & 255).astype(F32), 0.0)
    row = lax.broadcasted_iota(jnp.int32, (both, both), 0)
    col = lax.broadcasted_iota(jnp.int32, (both, both), 1)
    per = both // 2
    earlier = (row < col) & ((row >= per) == (col >= per))
    position = dot(member.astype(BF16), jnp.where(earlier, 1.0, 0.0).astype(BF16))
    key = jnp.where((member > 0.5) & (position < CAP - 0.5), position, -1.0)
    return key.astype(BF16), high.astype(BF16), low.astype(BF16)


def slots(routed, group, core, quarter):
    key, high, low = routed
    experts, both = key.shape
    rows = quarter * 2 * CAP
    row = lax.broadcasted_iota(jnp.int32, (rows, experts), 0)
    col = lax.broadcasted_iota(jnp.int32, (rows, experts), 1)
    pick = jnp.where(col == (group * quarter + row // (2 * CAP)) * 2 + core, 1.0, 0.0).astype(BF16)
    row = lax.broadcasted_iota(jnp.int32, (rows, both), 0)
    col = lax.broadcasted_iota(jnp.int32, (rows, both), 1)
    hit = (dot(pick, key) == (row % CAP).astype(F32)) & (
        ((row // CAP) % 2 == 1) == (col >= both // 2)
    )
    return (
        jnp.where(hit, 1.0, 0.0),
        jnp.where(hit, dot(pick, high) / 256.0, 0.0),
        jnp.where(hit, dot(pick, low) / 65536.0, 0.0),
    )


def kernel(
    experts,
    tokens, ids, gates, routed_w, shared_w,
    out,
    tok, meta, sel0, sel1, c0h, c0l, c1h, c1l, msg, arr, wgu, wd, gu, hid, shd, part, yred,
    rets, retc, sibs, sibr, yfs, yfr, keep,
    load_sem, meta_s, meta_r, tsib_s, tsib_r, ty_s, ty_r, tdi_s, tdi_r,
    dc_s, dc_r, d0_s, d0_r, d1_s, d1_r, fw_s, fw_r,
    yr_s, yr_r, r0_s, r0_r, r1_s, r1_r, rc_s, rc_r, sb_s, sb_r, yf_s, yf_r,
):
    ep, y = lax.axis_index("ep"), lax.axis_index("tp")
    core, place = lax.rem(ep, 2), ep // 2
    quarter = experts // 4
    half, q = place // quarter, lax.rem(place, quarter)
    per, width = tokens.shape
    tops = ids.shape[0]
    block = 2 * CAP
    hidden = wd.shape[1]
    sib, ypart, diag = (ep + 1 - 2 * core, y), (ep, 1 - y), (ep + 1 - 2 * core, 1 - y)

    def near(r):
        return lax.rem(q + r, quarter)

    def near_dev(r):
        return ((half * quarter + near(r)) * 2 + core, y)

    def far_dev(r):
        return (((1 - half) * quarter + near(r)) * 2 + core, y)

    def rows(index):
        return pl.ds(pl.multiple_of(index * block, block), block)

    def send(src, dst, s, r, dev):
        return pltpu.make_async_remote_copy(
            src_ref=src, dst_ref=dst, send_sem=s, recv_sem=r, device_id=dev, device_id_type=MESH
        )

    def columns(first, length):
        return pl.ds(first, length)

    own_tokens = pltpu.make_async_copy(tokens, tok.at[0, 0], load_sem.at[0])
    own_tokens.start()
    shared_gu = pltpu.make_async_copy(shared_w.at[pl.ds(0, 2)], wgu, load_sem.at[1])
    shared_d = pltpu.make_async_copy(shared_w.at[2], wd, load_sem.at[2])
    shared_gu.start()
    shared_d.start()
    meta[0, pl.ds(0, tops), :] = ids[...]
    meta[0, pl.ds(tops, tops), :] = gates[...]

    barrier = pltpu.get_barrier_semaphore()
    peers = [sib, ypart, diag]
    peers += [near_dev(r) for r in range(1, quarter)] + [far_dev(r) for r in range(quarter)]
    for peer in peers:
        pl.semaphore_signal(barrier, inc=1, device_id=peer, device_id_type=MESH)
    pl.semaphore_wait(barrier, len(peers))

    pending = []

    def go(copy):
        copy.start()
        pending.append(copy)
        return copy

    metas = [
        go(send(meta.at[0], meta.at[k], meta_s.at[k], meta_r.at[k], dev))
        for k, dev in ((1, sib), (2, ypart), (3, diag))
    ]
    own_tokens.wait()
    span = width // SPANS
    tsib, ty = [], []
    for d in range(SPANS):
        at = columns(d * span, span)
        src = tok.at[0, 0, :, at]
        tsib.append(go(send(src, tok.at[0, 1, :, at], tsib_s.at[d], tsib_r.at[d], sib)))
    for d in range(SPANS):
        at = columns(d * span, span)
        src = tok.at[0, 0, :, at]
        ty.append(go(send(src, tok.at[1, 0, :, at], ty_s.at[d], ty_r.at[d], ypart)))

    metas[0].wait_recv()
    routed = routing(jnp.concatenate([meta[0], meta[1]], axis=1), experts)
    far, far_h, far_l = slots(routed, 1 - half, core, quarter)
    here, here_h, here_l = slots(routed, half, core, quarter)
    sel0[...] = jnp.concatenate([far, here], axis=0).astype(BF16)
    c0h[...] = jnp.concatenate([far_h, here_h], axis=0).T.astype(BF16)
    c0l[...] = jnp.concatenate([far_l, here_l], axis=0).T.astype(BF16)
    dcross, dnear0, dnear1 = [], [], []
    nrow = quarter * block
    for d in range(SPANS):
        tsib[d].wait_recv()

        @pl.loop(0, span // STEP)
        def _(i):
            at = pl.ds(pl.multiple_of(d * span + i * STEP, STEP), STEP)
            got = dot(sel0[...], tok[0, :, :, at].reshape(2 * per, STEP)).astype(BF16)
            msg[0, :, at] = got[:nrow]
            msg[1, :, at] = got[nrow:]

        at = columns(d * span, span)
        for r in range(quarter):
            dcross.append(go(send(
                msg.at[0, rows(near(r)), at], arr.at[2, rows(q), at],
                dc_s.at[d, r], dc_r.at[d, r], far_dev(r),
            )))
        for r in range(1, quarter):
            dnear0.append(go(send(
                msg.at[1, rows(near(r)), at], arr.at[0, rows(q), at],
                d0_s.at[d, r], d0_r.at[d, r], near_dev(r),
            )))
    arr[0, rows(q), :] = msg[1, rows(q), :]

    metas[1].wait_recv()
    metas[2].wait_recv()
    routed = routing(jnp.concatenate([meta[2], meta[3]], axis=1), experts)
    here, here_h, here_l = slots(routed, half, core, quarter)
    sel1[...] = here.astype(BF16)
    c1h[...] = here_h.T.astype(BF16)
    c1l[...] = here_l.T.astype(BF16)
    tdi = []
    for d in range(SPANS):
        ty[d].wait_recv()
        at = columns(d * span, span)
        tdi.append(go(send(
            tok.at[1, 0, :, at], tok.at[1, 1, :, at], tdi_s.at[d], tdi_r.at[d], sib
        )))
    for d in range(SPANS):
        tdi[d].wait_recv()

        @pl.loop(0, span // STEP)
        def _(i):
            at = pl.ds(pl.multiple_of(d * span + i * STEP, STEP), STEP)
            got = dot(sel1[...], tok[1, :, :, at].reshape(2 * per, STEP)).astype(BF16)
            msg[2, :, at] = got

        at = columns(d * span, span)
        for r in range(1, quarter):
            dnear1.append(go(send(
                msg.at[2, rows(near(r)), at], arr.at[1, rows(q), at],
                d1_s.at[d, r], d1_r.at[d, r], near_dev(r),
            )))
    arr[1, rows(q), :] = msg[2, rows(q), :]

    def up(read, count):
        gu[...] = jnp.zeros_like(gu)

        @pl.loop(0, width // DEPTH)
        def _(i):
            at = pl.ds(pl.multiple_of(i * DEPTH, DEPTH), DEPTH)
            x = read(at)
            gu[0, pl.ds(0, count), :] += dot(x, wgu[0, at, :])
            gu[1, pl.ds(0, count), :] += dot(x, wgu[1, at, :])

        gate = gu[0, pl.ds(0, count), :]
        hid[pl.ds(0, count), :] = (
            gate / (1.0 + jnp.exp(-gate)) * gu[1, pl.ds(0, count), :]
        ).astype(BF16)

    forwards = []

    def forward(d):
        at = columns(d * span, span)
        for r in range(quarter):
            dcross[d * quarter + r].wait_recv()
            src = lax.rem(q + quarter - r, quarter)
            forwards.append(go(send(
                arr.at[2, rows(src), at], arr.at[3, rows(src), at],
                fw_s.at[d, r], fw_r.at[d, r], ypart,
            )))

    shared_gu.wait()
    up(lambda at: jnp.concatenate([tok[0, 0, :, at], tok[1, 0, :, at]], axis=0), 2 * per)
    routed_gu = pltpu.make_async_copy(routed_w.at[0, pl.ds(0, 2)], wgu, load_sem.at[1])
    routed_gu.start()
    forward(0)
    shared_d.wait()

    @pl.loop(0, width // STEP)
    def _(i):
        at = pl.ds(pl.multiple_of(i * STEP, STEP), STEP)
        got = dot_t(hid[pl.ds(0, 2 * per), :], wd[at, :]).astype(BF16)
        shd[0, :, at] = got[:per]
        shd[1, :, at] = got[per:]

    routed_d = pltpu.make_async_copy(routed_w.at[0, 2], wd, load_sem.at[2])
    routed_d.start()
    for d in range(1, SPANS):
        forward(d)

    for copy in dnear0 + dnear1 + forwards:
        copy.wait_recv()
    routed_gu.wait()
    up(lambda at: arr[:, :, at].reshape(4 * nrow, DEPTH), 4 * nrow)
    routed_d.wait()

    piece = width // PIECES
    yreds, near0, near1, cross = [], [], [], []

    def reduce(j):
        yreds[j].wait_recv()
        at = columns(j * piece, piece)

        @pl.loop(0, piece // STEP)
        def _(i):
            at = pl.ds(pl.multiple_of(j * piece + i * STEP, STEP), STEP)
            part[2, :, at] = (part[2, :, at].astype(F32) + yred[:, at].astype(F32)).astype(BF16)

        for r in range(quarter):
            cross.append(go(send(
                part.at[2, rows(near(r)), at], retc.at[rows(q), at],
                rc_s.at[j, r], rc_r.at[j, r], far_dev(r),
            )))

    for j in range(PIECES):
        @pl.loop(0, piece // STEP)
        def _(i):
            at = pl.ds(pl.multiple_of(j * piece + i * STEP, STEP), STEP)
            got = dot_t(hid[...], wd[at, :]).astype(BF16)
            part[:, :, at] = got.reshape(4, nrow, STEP)

        at = columns(j * piece, piece)
        yreds.append(go(send(part.at[3, :, at], yred.at[:, at], yr_s.at[j], yr_r.at[j], ypart)))
        for r in range(1, quarter):
            near1.append(go(send(
                part.at[1, rows(near(r)), at], rets.at[1, rows(q), at],
                r1_s.at[j, r], r1_r.at[j, r], near_dev(r),
            )))
        for r in range(1, quarter):
            near0.append(go(send(
                part.at[0, rows(near(r)), at], rets.at[0, rows(q), at],
                r0_s.at[j, r], r0_r.at[j, r], near_dev(r),
            )))
        if j > 0:
            reduce(j - 1)
    rets[0, rows(q), :] = part[0, rows(q), :]
    rets[1, rows(q), :] = part[1, rows(q), :]
    reduce(PIECES - 1)

    sums = [[], []]

    def to_sibling(dy, j):
        at = columns(j * piece, piece)
        sums[dy].append(go(send(
            sibs.at[dy, :, at], sibr.at[dy, :, at], sb_s.at[dy, j], sb_r.at[dy, j], sib
        )))

    for j in range(PIECES):
        for copy in near1[j * (quarter - 1) : (j + 1) * (quarter - 1)]:
            copy.wait_recv()

        @pl.loop(0, piece // STEP)
        def _(i):
            at = pl.ds(pl.multiple_of(j * piece + i * STEP, STEP), STEP)
            x = rets[1, :, at]
            got = dot(c1h[...], x) + dot(c1l[...], x)
            sibs[1, :, at] = got[per:].astype(BF16)
            keep[:, at] = got[:per] + shd[1, :, at].astype(F32)

        to_sibling(1, j)
    finals = []
    for j in range(PIECES):
        sums[1][j].wait_recv()

        @pl.loop(0, piece // STEP)
        def _(i):
            at = pl.ds(pl.multiple_of(j * piece + i * STEP, STEP), STEP)
            yfs[:, at] = (keep[:, at] + sibr[1, :, at].astype(F32)).astype(BF16)

        at = columns(j * piece, piece)
        finals.append(go(send(yfs.at[:, at], yfr.at[:, at], yf_s.at[j], yf_r.at[j], ypart)))

    for j in range(PIECES):
        for copy in near0[j * (quarter - 1) : (j + 1) * (quarter - 1)]:
            copy.wait_recv()
        for copy in cross[j * quarter : (j + 1) * quarter]:
            copy.wait_recv()

        @pl.loop(0, piece // STEP)
        def _(i):
            at = pl.ds(pl.multiple_of(j * piece + i * STEP, STEP), STEP)
            x = jnp.concatenate([retc[:, at], rets[0, :, at]], axis=0)
            got = dot(c0h[...], x) + dot(c0l[...], x)
            sibs[0, :, at] = got[per:].astype(BF16)
            keep[:, at] = got[:per] + shd[0, :, at].astype(F32)

        to_sibling(0, j)
    for j in range(PIECES):
        sums[0][j].wait_recv()
        finals[j].wait_recv()

        @pl.loop(0, piece // STEP)
        def _(i):
            at = pl.ds(pl.multiple_of(j * piece + i * STEP, STEP), STEP)
            out[:, at] = (
                keep[:, at] + sibr[0, :, at].astype(F32) + yfr[:, at].astype(F32)
            ).astype(BF16)

    for copy in pending:
        copy.wait_send()


def fused(tokens, expert_ids, gate_fixed, expert_weights, shared_weights):
    experts = lax.axis_size("ep")
    per, width = tokens.shape
    tops = expert_ids.shape[1]
    hidden = shared_weights.shape[2]
    quarter = experts // 4
    nrow = quarter * 2 * CAP
    vmem = pltpu.VMEM
    dma = pltpu.SemaphoreType.DMA
    hbm = pl.BlockSpec(memory_space=pl.ANY)
    near = pl.BlockSpec(memory_space=pltpu.VMEM)

    def pair(*shape):
        return [dma(shape), dma(shape)]

    scratch = [
        vmem((2, 2, per, width), BF16),
        vmem((4, 2 * tops, per), jnp.int32),
        vmem((2 * nrow, 2 * per), BF16),
        vmem((nrow, 2 * per), BF16),
        vmem((2 * per, 2 * nrow), BF16),
        vmem((2 * per, 2 * nrow), BF16),
        vmem((2 * per, nrow), BF16),
        vmem((2 * per, nrow), BF16),
        vmem((3, nrow, width), BF16),
        vmem((4, nrow, width), BF16),
        vmem((2, width, hidden), BF16),
        vmem((width, hidden), BF16),
        vmem((2, 4 * nrow, hidden), F32),
        vmem((4 * nrow, hidden), BF16),
        vmem((2, per, width), BF16),
        vmem((4, nrow, width), BF16),
        vmem((nrow, width), BF16),
        vmem((2, nrow, width), BF16),
        vmem((nrow, width), BF16),
        vmem((2, per, width), BF16),
        vmem((2, per, width), BF16),
        vmem((per, width), BF16),
        vmem((per, width), BF16),
        vmem((per, width), F32),
        dma((3,)),
    ]
    scratch += pair(4) + pair(SPANS) + pair(SPANS) + pair(SPANS)
    scratch += pair(SPANS, quarter) * 4
    scratch += pair(PIECES) + pair(PIECES, quarter) * 3 + pair(2, PIECES) + pair(PIECES)
    return pl.pallas_call(
        functools.partial(kernel, experts),
        out_shape=jax.ShapeDtypeStruct((per, width), BF16),
        in_specs=[hbm, near, near, hbm, hbm],
        out_specs=near,
        scratch_shapes=scratch,
        compiler_params=pltpu.CompilerParams(
            collective_id=0, has_side_effects=True, vmem_limit_bytes=60 * 1024 * 1024
        ),
        cost_estimate=pl.CostEstimate(
            flops=2 * 3 * (4 * nrow + 2 * per) * width * hidden,
            bytes_accessed=2 * 6 * width * hidden,
            transcendentals=0,
        ),
    )(tokens, expert_ids.T, gate_fixed.T, expert_weights, shared_weights)


def local_part(inputs, weights):
    gate_proj = jnp.dot(inputs, weights[0], preferred_element_type=F32)
    up_proj = jnp.dot(inputs, weights[1], preferred_element_type=F32)
    hidden = (jax.nn.silu(gate_proj) * up_proj).astype(BF16)
    return dot_t(hidden, weights[2])


def general(tokens, expert_ids, gate_fixed, expert_weights, shared_weights):
    per_dev = tokens.shape[0]
    width = tokens.shape[1]
    expert_count = lax.axis_size("ep")
    tp_count = lax.axis_size("tp")
    own_weights = expert_weights[0]
    expert_range = jnp.arange(expert_count, dtype=jnp.int32)
    match = expert_ids[:, :, None] == expert_range[None, None, :]
    member = jnp.sum(match.astype(jnp.int32), axis=1)
    position = jnp.cumsum(member, axis=0) - member
    kept = member * (position < CAP).astype(jnp.int32)
    slot_range = jnp.arange(CAP, dtype=jnp.int32)
    hit = (kept[:, :, None] == 1) & (position[:, :, None] == slot_range[None, None, :])
    select = hit.astype(BF16).reshape(per_dev, expert_count * CAP)
    outgoing = jnp.einsum("tk,td->kd", select, tokens, preferred_element_type=F32)
    outgoing = outgoing.astype(BF16).reshape(expert_count, CAP, width)
    widened = jnp.broadcast_to(outgoing[:, None], (expert_count, tp_count, CAP, width))
    widened = widened.reshape(expert_count * tp_count, CAP, width)
    arrived = lax.all_to_all(widened, ("ep", "tp"), split_axis=0, concat_axis=0, tiled=True)
    senders = arrived.shape[0]
    slots_here = arrived.shape[1]
    part_out = local_part(arrived.reshape(-1, width), own_weights)
    part_out = part_out.astype(BF16).reshape(senders, slots_here, width)
    parts_back = lax.all_to_all(part_out, ("ep", "tp"), split_axis=0, concat_axis=0, tiled=True)
    parts_back = parts_back.reshape(expert_count, tp_count, CAP, width).astype(F32)
    returned = jnp.sum(parts_back, axis=1).astype(BF16)
    slot_pos = jnp.sum(jnp.where(match, position[:, None, :], 0), axis=2)
    slot_keep = slot_pos < CAP
    slot_index = jnp.where(slot_keep, expert_ids * CAP + slot_pos, 0)
    slot_rows = returned.reshape(expert_count * CAP, width)[slot_index]
    slot_gate = jnp.where(slot_keep, gate_fixed.astype(F32) / 65536.0, 0.0)
    routed = jnp.sum(slot_gate[:, :, None] * slot_rows.astype(F32), axis=1)
    shared_terms = local_part(lax.all_gather(tokens, "tp", axis=0, tiled=True), shared_weights)
    shared = lax.psum_scatter(
        shared_terms.astype(BF16), "tp", scatter_dimension=0, tiled=True
    ).astype(F32)
    return (shared + routed).astype(BF16)


def solution(mesh):
    placed = (
        P(("ep", "tp"), None),
        P(("ep", "tp"), None),
        P(("ep", "tp"), None),
        P("ep", None, None, "tp"),
        P(None, None, "tp"),
    )
    body = fused if mesh.shape["tp"] == 2 and mesh.shape["ep"] == 16 else general
    return jax.shard_map(
        body, mesh=mesh, in_specs=placed, out_specs=P(("ep", "tp"), None), check_vma=False
    )
```

```python
import functools

import jax
import jax.numpy as jnp
from jax import lax
from jax.experimental import pallas as pl
from jax.experimental.pallas import tpu as pltpu
from jax.sharding import PartitionSpec as P

CAP = 8
MESH = pl.DeviceIdType.MESH
BF16 = jnp.bfloat16
F32 = jnp.float32

SPANS = 4
PIECES = 4
STEP = 256
DEPTH = 1024


def dot(a, b):
    return jnp.dot(a, b, preferred_element_type=F32)


def dot_t(a, b):
    return lax.dot_general(a, b, (((1,), (1,)), ((), ())), preferred_element_type=F32)


def routing(meta, experts):
    tops = meta.shape[0] // 2
    both = meta.shape[1]
    expert = lax.broadcasted_iota(jnp.int32, (experts, both), 0)
    member = jnp.zeros((experts, both), F32)
    high = jnp.zeros((experts, both), F32)
    low = jnp.zeros((experts, both), F32)
    for k in range(tops):
        match = meta[k : k + 1, :] == expert
        gate = meta[tops + k : tops + k + 1, :]
        member += jnp.where(match, 1.0, 0.0)
        high += jnp.where(match, (gate >> 8).astype(F32), 0.0)
        low += jnp.where(match, (gate & 255).astype(F32), 0.0)
    row = lax.broadcasted_iota(jnp.int32, (both, both), 0)
    col = lax.broadcasted_iota(jnp.int32, (both, both), 1)
    per = both // 2
    earlier = (row < col) & ((row >= per) == (col >= per))
    position = dot(member.astype(BF16), jnp.where(earlier, 1.0, 0.0).astype(BF16))
    key = jnp.where((member > 0.5) & (position < CAP - 0.5), position, -1.0)
    return key.astype(BF16), high.astype(BF16), low.astype(BF16)


def slots(routed, group, core, quarter):
    key, high, low = routed
    experts, both = key.shape
    rows = quarter * 2 * CAP
    row = lax.broadcasted_iota(jnp.int32, (rows, experts), 0)
    col = lax.broadcasted_iota(jnp.int32, (rows, experts), 1)
    pick = jnp.where(col == (group * quarter + row // (2 * CAP)) * 2 + core, 1.0, 0.0).astype(BF16)
    row = lax.broadcasted_iota(jnp.int32, (rows, both), 0)
    col = lax.broadcasted_iota(jnp.int32, (rows, both), 1)
    hit = (dot(pick, key) == (row % CAP).astype(F32)) & (
        ((row // CAP) % 2 == 1) == (col >= both // 2)
    )
    return (
        jnp.where(hit, 1.0, 0.0),
        jnp.where(hit, dot(pick, high) / 256.0, 0.0),
        jnp.where(hit, dot(pick, low) / 65536.0, 0.0),
    )


def kernel(
    experts,
    tokens, ids, gates, routed_w, shared_w,
    out,
    tok, meta, sel0, sel1, c0h, c0l, c1h, c1l, msg, arr, wgu, wd, gu, hid, shd, part, yred,
    rets, retc, sibs, sibr, yfs, yfr, keep,
    load_sem, meta_s, meta_r, tsib_s, tsib_r, ty_s, ty_r, tdi_s, tdi_r,
    dc_s, dc_r, d0_s, d0_r, d1_s, d1_r, fw_s, fw_r,
    yr_s, yr_r, r0_s, r0_r, r1_s, r1_r, rc_s, rc_r, sb_s, sb_r, yf_s, yf_r,
):
    ep, y = lax.axis_index("ep"), lax.axis_index("tp")
    core, place = lax.rem(ep, 2), ep // 2
    quarter = experts // 4
    half, q = place // quarter, lax.rem(place, quarter)
    per, width = tokens.shape
    tops = ids.shape[0]
    block = 2 * CAP
    sib, ypart, diag = (ep + 1 - 2 * core, y), (ep, 1 - y), (ep + 1 - 2 * core, 1 - y)

    def near(r):
        return lax.rem(q + r, quarter)

    def near_dev(r):
        return ((half * quarter + near(r)) * 2 + core, y)

    def far_dev(r):
        return (((1 - half) * quarter + near(r)) * 2 + core, y)

    def back_dev(r):
        return (((1 - half) * quarter + near(quarter - r)) * 2 + core, y)

    nrow = quarter * block
    group = quarter // 2

    def own_rows(r):
        return pl.ds((r // group) * 2 * nrow + nrow + (r % group) * block, block)

    def passed_rows(r):
        return pl.ds((r // group) * 2 * nrow + nrow + (group + r % group) * block, block)

    def near_rows(b, index):
        return pl.ds(pl.multiple_of(b * 2 * nrow + index * block, block), block)

    def rows(index):
        return pl.ds(pl.multiple_of(index * block, block), block)

    def send(src, dst, s, r, dev):
        return pltpu.make_async_remote_copy(
            src_ref=src, dst_ref=dst, send_sem=s, recv_sem=r, device_id=dev, device_id_type=MESH
        )

    def columns(first, length):
        return pl.ds(first, length)

    own_tokens = pltpu.make_async_copy(tokens, tok.at[0, 0], load_sem.at[0])
    own_tokens.start()
    shared_gu = pltpu.make_async_copy(shared_w.at[pl.ds(0, 2)], wgu, load_sem.at[1])
    shared_d = pltpu.make_async_copy(shared_w.at[2], wd, load_sem.at[2])
    shared_gu.start()
    shared_d.start()
    meta[0, pl.ds(0, tops), :] = ids[...]
    meta[0, pl.ds(tops, tops), :] = gates[...]

    barrier = pltpu.get_barrier_semaphore()
    peers = [sib, ypart, diag]
    peers += [near_dev(r) for r in range(1, quarter)] + [far_dev(r) for r in range(quarter)]
    for peer in peers:
        pl.semaphore_signal(barrier, inc=1, device_id=peer, device_id_type=MESH)
    pl.semaphore_wait(barrier, len(peers))

    pending = []

    def go(copy):
        copy.start()
        pending.append(copy)
        return copy

    metas = [
        go(send(meta.at[0], meta.at[k], meta_s.at[k], meta_r.at[k], dev))
        for k, dev in ((1, sib), (2, ypart), (3, diag))
    ]
    own_tokens.wait()
    span = width // SPANS
    tsib, ty = [], []
    for d in range(SPANS):
        at = columns(d * span, span)
        src = tok.at[0, 0, :, at]
        tsib.append(go(send(src, tok.at[0, 1, :, at], tsib_s.at[d], tsib_r.at[d], sib)))
    for d in range(SPANS):
        at = columns(d * span, span)
        src = tok.at[0, 0, :, at]
        ty.append(go(send(src, tok.at[1, 0, :, at], ty_s.at[d], ty_r.at[d], ypart)))

    metas[0].wait_recv()
    routed = routing(jnp.concatenate([meta[0], meta[1]], axis=1), experts)
    far, far_h, far_l = slots(routed, 1 - half, core, quarter)
    here, here_h, here_l = slots(routed, half, core, quarter)
    sel0[...] = jnp.concatenate([far, here], axis=0).astype(BF16)
    c0h[...] = jnp.concatenate([far_h, here_h], axis=0).T.astype(BF16)
    c0l[...] = jnp.concatenate([far_l, here_l], axis=0).T.astype(BF16)
    dcross, dnear0, dnear1 = {}, [], []

    def send_far(d, b):
        at = columns(d * span, span)
        for r in range(b * group, (b + 1) * group):
            dcross[d, r] = go(send(
                msg.at[0, rows(near(r)), at], arr.at[own_rows(r), at],
                dc_s.at[d, r], dc_r.at[d, r], far_dev(r),
            ))

    for d in range(SPANS):
        tsib[d].wait_recv()

        @pl.loop(0, span // STEP)
        def _(i):
            at = pl.ds(pl.multiple_of(d * span + i * STEP, STEP), STEP)
            got = dot(sel0[...], tok[0, :, :, at].reshape(2 * per, STEP)).astype(BF16)
            msg[0, :, at] = got[:nrow]
            msg[1, :, at] = got[nrow:]

        send_far(d, 0)
        at = columns(d * span, span)
        for r in range(1, quarter):
            dnear0.append(go(send(
                msg.at[1, rows(near(r)), at], arr.at[near_rows(0, q), at],
                d0_s.at[d, r], d0_r.at[d, r], near_dev(r),
            )))
    for d in range(SPANS):
        send_far(d, 1)
    arr[near_rows(0, q), :] = msg[1, rows(q), :]

    metas[1].wait_recv()
    metas[2].wait_recv()
    routed = routing(jnp.concatenate([meta[2], meta[3]], axis=1), experts)
    here, here_h, here_l = slots(routed, half, core, quarter)
    sel1[...] = here.astype(BF16)
    c1h[...] = here_h.T.astype(BF16)
    c1l[...] = here_l.T.astype(BF16)
    tdi = []
    for d in range(SPANS):
        ty[d].wait_recv()
        at = columns(d * span, span)
        tdi.append(go(send(
            tok.at[1, 0, :, at], tok.at[1, 1, :, at], tdi_s.at[d], tdi_r.at[d], sib
        )))
    for d in range(SPANS):
        tdi[d].wait_recv()

        @pl.loop(0, span // STEP)
        def _(i):
            at = pl.ds(pl.multiple_of(d * span + i * STEP, STEP), STEP)
            got = dot(sel1[...], tok[1, :, :, at].reshape(2 * per, STEP)).astype(BF16)
            msg[2, :, at] = got

        at = columns(d * span, span)
        for r in range(1, quarter):
            dnear1.append(go(send(
                msg.at[2, rows(near(r)), at], arr.at[near_rows(1, q), at],
                d1_s.at[d, r], d1_r.at[d, r], near_dev(r),
            )))
    arr[near_rows(1, q), :] = msg[2, rows(q), :]

    def up(read, count):
        gu[...] = jnp.zeros_like(gu)

        @pl.loop(0, width // DEPTH)
        def _(i):
            at = pl.ds(pl.multiple_of(i * DEPTH, DEPTH), DEPTH)
            x = read(at)
            gu[0, pl.ds(0, count), :] += dot(x, wgu[0, at, :])
            gu[1, pl.ds(0, count), :] += dot(x, wgu[1, at, :])

        gate = gu[0, pl.ds(0, count), :]
        hid[pl.ds(0, count), :] = (
            gate / (1.0 + jnp.exp(-gate)) * gu[1, pl.ds(0, count), :]
        ).astype(BF16)

    forwards = [[], []]

    def forward(d, b):
        at = columns(d * span, span)
        for r in range(b * group, (b + 1) * group):
            dcross[d, r].wait_recv()
            forwards[b].append(go(send(
                arr.at[own_rows(r), at], arr.at[passed_rows(r), at],
                fw_s.at[d, r], fw_r.at[d, r], ypart,
            )))

    for d in range(SPANS):
        forward(d, 0)
    shared_gu.wait()
    up(lambda at: jnp.concatenate([tok[0, 0, :, at], tok[1, 0, :, at]], axis=0), 2 * per)
    routed_gu = pltpu.make_async_copy(routed_w.at[0, pl.ds(0, 2)], wgu, load_sem.at[1])
    routed_gu.start()
    shared_d.wait()

    @pl.loop(0, width // STEP)
    def _(i):
        at = pl.ds(pl.multiple_of(i * STEP, STEP), STEP)
        got = dot_t(hid[pl.ds(0, 2 * per), :], wd[at, :]).astype(BF16)
        shd[0, :, at] = got[:per]
        shd[1, :, at] = got[per:]

    routed_d = pltpu.make_async_copy(routed_w.at[0, 2], wd, load_sem.at[2])
    routed_d.start()

    piece = width // PIECES
    batch = 2 * nrow
    yreds, near0, near1, cross = {}, [], [], {}
    hrow = group * block

    def reduce(b, j):
        yreds[b, j].wait_recv()
        at = columns(j * piece, piece)
        own = pl.ds(b * batch + nrow, hrow)

        @pl.loop(0, piece // STEP)
        def _(i):
            at = pl.ds(pl.multiple_of(j * piece + i * STEP, STEP), STEP)
            part[own, at] = (
                part[own, at].astype(F32) + yred[pl.ds(b * hrow, hrow), at].astype(F32)
            ).astype(BF16)

        for r in range(b * group, (b + 1) * group):
            cross[j, r] = go(send(
                part.at[own_rows(r), at], retc.at[rows(q), at],
                rc_s.at[j, r], rc_r.at[j, r], back_dev(r),
            ))

    def down(b, j):
        @pl.loop(0, piece // STEP)
        def _(i):
            at = pl.ds(pl.multiple_of(j * piece + i * STEP, STEP), STEP)
            part[pl.ds(b * batch, batch), at] = dot_t(hid[...], wd[at, :]).astype(BF16)

        at = columns(j * piece, piece)
        yreds[b, j] = go(send(
            part.at[pl.ds(b * batch + nrow + hrow, hrow), at], yred.at[pl.ds(b * hrow, hrow), at],
            yr_s.at[b, j], yr_r.at[b, j], ypart,
        ))
        returned, s, r_ = (near0, r0_s, r0_r) if b == 0 else (near1, r1_s, r1_r)
        for r in range(1, quarter):
            returned.append(go(send(
                part.at[near_rows(b, near(r)), at], rets.at[b, rows(q), at],
                s.at[j, r], r_.at[j, r], near_dev(r),
            )))

    for b in range(2):
        for copy in (dnear0, dnear1)[b] + forwards[b]:
            copy.wait_recv()
        if b == 0:
            routed_gu.wait()
        up(lambda at: arr[pl.ds(b * batch, batch), at], batch)
        if b == 0:
            routed_d.wait()
        for j in range(PIECES):
            down(b, j)
            if b == 0:
                for d in range(j * SPANS // PIECES, (j + 1) * SPANS // PIECES):
                    forward(d, 1)
            if j > 0:
                reduce(b, j - 1)
        rets[b, rows(q), :] = part[near_rows(b, q), :]
        reduce(b, PIECES - 1)

    sums = [[], []]

    def to_sibling(dy, j):
        at = columns(j * piece, piece)
        sums[dy].append(go(send(
            sibs.at[dy, :, at], sibr.at[dy, :, at], sb_s.at[dy, j], sb_r.at[dy, j], sib
        )))

    for j in range(PIECES):
        for copy in near1[j * (quarter - 1) : (j + 1) * (quarter - 1)]:
            copy.wait_recv()

        @pl.loop(0, piece // STEP)
        def _(i):
            at = pl.ds(pl.multiple_of(j * piece + i * STEP, STEP), STEP)
            x = rets[1, :, at]
            got = dot(c1h[...], x) + dot(c1l[...], x)
            sibs[1, :, at] = got[per:].astype(BF16)
            keep[:, at] = got[:per] + shd[1, :, at].astype(F32)

        to_sibling(1, j)
    finals = []
    for j in range(PIECES):
        sums[1][j].wait_recv()

        @pl.loop(0, piece // STEP)
        def _(i):
            at = pl.ds(pl.multiple_of(j * piece + i * STEP, STEP), STEP)
            yfs[:, at] = (keep[:, at] + sibr[1, :, at].astype(F32)).astype(BF16)

        at = columns(j * piece, piece)
        finals.append(go(send(yfs.at[:, at], yfr.at[:, at], yf_s.at[j], yf_r.at[j], ypart)))

    for j in range(PIECES):
        for copy in near0[j * (quarter - 1) : (j + 1) * (quarter - 1)]:
            copy.wait_recv()
        for r in range(quarter):
            cross[j, r].wait_recv()

        @pl.loop(0, piece // STEP)
        def _(i):
            at = pl.ds(pl.multiple_of(j * piece + i * STEP, STEP), STEP)
            x = jnp.concatenate([retc[:, at], rets[0, :, at]], axis=0)
            got = dot(c0h[...], x) + dot(c0l[...], x)
            sibs[0, :, at] = got[per:].astype(BF16)
            keep[:, at] = got[:per] + shd[0, :, at].astype(F32)

        to_sibling(0, j)
    for j in range(PIECES):
        sums[0][j].wait_recv()
        finals[j].wait_recv()

        @pl.loop(0, piece // STEP)
        def _(i):
            at = pl.ds(pl.multiple_of(j * piece + i * STEP, STEP), STEP)
            out[:, at] = (
                keep[:, at] + sibr[0, :, at].astype(F32) + yfr[:, at].astype(F32)
            ).astype(BF16)

    for copy in pending:
        copy.wait_send()


def fused(tokens, expert_ids, gate_fixed, expert_weights, shared_weights):
    experts = lax.axis_size("ep")
    per, width = tokens.shape
    tops = expert_ids.shape[1]
    hidden = shared_weights.shape[2]
    quarter = experts // 4
    nrow = quarter * 2 * CAP
    vmem = pltpu.VMEM
    dma = pltpu.SemaphoreType.DMA
    hbm = pl.BlockSpec(memory_space=pl.ANY)
    near = pl.BlockSpec(memory_space=pltpu.VMEM)

    def pair(*shape):
        return [dma(shape), dma(shape)]

    scratch = [
        vmem((2, 2, per, width), BF16),
        vmem((4, 2 * tops, per), jnp.int32),
        vmem((2 * nrow, 2 * per), BF16),
        vmem((nrow, 2 * per), BF16),
        vmem((2 * per, 2 * nrow), BF16),
        vmem((2 * per, 2 * nrow), BF16),
        vmem((2 * per, nrow), BF16),
        vmem((2 * per, nrow), BF16),
        vmem((3, nrow, width), BF16),
        vmem((4 * nrow, width), BF16),
        vmem((2, width, hidden), BF16),
        vmem((width, hidden), BF16),
        vmem((2, 2 * nrow, hidden), F32),
        vmem((2 * nrow, hidden), BF16),
        vmem((2, per, width), BF16),
        vmem((4 * nrow, width), BF16),
        vmem((nrow, width), BF16),
        vmem((2, nrow, width), BF16),
        vmem((nrow, width), BF16),
        vmem((2, per, width), BF16),
        vmem((2, per, width), BF16),
        vmem((per, width), BF16),
        vmem((per, width), BF16),
        vmem((per, width), F32),
        dma((3,)),
    ]
    scratch += pair(4) + pair(SPANS) + pair(SPANS) + pair(SPANS)
    scratch += pair(SPANS, quarter) * 4
    scratch += pair(2, PIECES) + pair(PIECES, quarter) * 3 + pair(2, PIECES) + pair(PIECES)
    return pl.pallas_call(
        functools.partial(kernel, experts),
        out_shape=jax.ShapeDtypeStruct((per, width), BF16),
        in_specs=[hbm, near, near, hbm, hbm],
        out_specs=near,
        scratch_shapes=scratch,
        compiler_params=pltpu.CompilerParams(
            collective_id=0, has_side_effects=True, vmem_limit_bytes=60 * 1024 * 1024
        ),
        cost_estimate=pl.CostEstimate(
            flops=2 * 3 * (4 * nrow + 2 * per) * width * hidden,
            bytes_accessed=2 * 6 * width * hidden,
            transcendentals=0,
        ),
    )(tokens, expert_ids.T, gate_fixed.T, expert_weights, shared_weights)


def local_part(inputs, weights):
    gate_proj = jnp.dot(inputs, weights[0], preferred_element_type=F32)
    up_proj = jnp.dot(inputs, weights[1], preferred_element_type=F32)
    hidden = (jax.nn.silu(gate_proj) * up_proj).astype(BF16)
    return dot_t(hidden, weights[2])


def general(tokens, expert_ids, gate_fixed, expert_weights, shared_weights):
    per_dev = tokens.shape[0]
    width = tokens.shape[1]
    expert_count = lax.axis_size("ep")
    tp_count = lax.axis_size("tp")
    own_weights = expert_weights[0]
    expert_range = jnp.arange(expert_count, dtype=jnp.int32)
    match = expert_ids[:, :, None] == expert_range[None, None, :]
    member = jnp.sum(match.astype(jnp.int32), axis=1)
    position = jnp.cumsum(member, axis=0) - member
    kept = member * (position < CAP).astype(jnp.int32)
    slot_range = jnp.arange(CAP, dtype=jnp.int32)
    hit = (kept[:, :, None] == 1) & (position[:, :, None] == slot_range[None, None, :])
    select = hit.astype(BF16).reshape(per_dev, expert_count * CAP)
    outgoing = jnp.einsum("tk,td->kd", select, tokens, preferred_element_type=F32)
    outgoing = outgoing.astype(BF16).reshape(expert_count, CAP, width)
    widened = jnp.broadcast_to(outgoing[:, None], (expert_count, tp_count, CAP, width))
    widened = widened.reshape(expert_count * tp_count, CAP, width)
    arrived = lax.all_to_all(widened, ("ep", "tp"), split_axis=0, concat_axis=0, tiled=True)
    senders = arrived.shape[0]
    slots_here = arrived.shape[1]
    part_out = local_part(arrived.reshape(-1, width), own_weights)
    part_out = part_out.astype(BF16).reshape(senders, slots_here, width)
    parts_back = lax.all_to_all(part_out, ("ep", "tp"), split_axis=0, concat_axis=0, tiled=True)
    parts_back = parts_back.reshape(expert_count, tp_count, CAP, width).astype(F32)
    returned = jnp.sum(parts_back, axis=1).astype(BF16)
    slot_pos = jnp.sum(jnp.where(match, position[:, None, :], 0), axis=2)
    slot_keep = slot_pos < CAP
    slot_index = jnp.where(slot_keep, expert_ids * CAP + slot_pos, 0)
    slot_rows = returned.reshape(expert_count * CAP, width)[slot_index]
    slot_gate = jnp.where(slot_keep, gate_fixed.astype(F32) / 65536.0, 0.0)
    routed = jnp.sum(slot_gate[:, :, None] * slot_rows.astype(F32), axis=1)
    shared_terms = local_part(lax.all_gather(tokens, "tp", axis=0, tiled=True), shared_weights)
    shared = lax.psum_scatter(
        shared_terms.astype(BF16), "tp", scatter_dimension=0, tiled=True
    ).astype(F32)
    return (shared + routed).astype(BF16)


def solution(mesh):
    placed = (
        P(("ep", "tp"), None),
        P(("ep", "tp"), None),
        P(("ep", "tp"), None),
        P("ep", None, None, "tp"),
        P(None, None, "tp"),
    )
    body = fused if mesh.shape["tp"] == 2 and mesh.shape["ep"] == 16 else general
    return jax.shard_map(
        body, mesh=mesh, in_specs=placed, out_specs=P(("ep", "tp"), None), check_vma=False
    )
```
